128 devices in a mesh: section: 2 (over core), dp: 64 (over x, z, y).
Axes of the slice: x: 4, y: 4, z: 4, core: 2. Of those that a mesh axis runs over, the one named last changes fastest.
Arguments:
- inputs: bfloat16 [2, 8192, 1024], P(None, 'dp'), may hold values from -6 to 6
- cotangent: bfloat16 [2, 8192, 1024], P(None, 'dp'), may hold values from -6 to 6
- seq_lengths: int32 [2, 128], P(None, 'dp'), may hold values from 16 to 112, as said below
- norm_gain: bfloat16 [2, 1024], P('section', 'dp'), may hold values from 0.5 to 1.5
- in_weight: bfloat16 [2, 1024, 4384], P('section', 'dp'), may hold values from -0.1875 to 0.1875
- conv_weight: bfloat16 [2, 4, 2304], P('section', None, 'dp'), may hold values from -3 to 3
- conv_bias: bfloat16 [2, 2304], P('section', 'dp'), may hold values from -0.5 to 0.5
- dt_bias: bfloat16 [2, 32], P('section'), may hold values from -6 to -2
- a_log: bfloat16 [2, 32], P('section'), may hold values from 0 to 2.796875
- skip_gain: bfloat16 [2, 32], P('section'), may hold values from 0.5 to 1.5
- gate_gain: bfloat16 [2, 2048], P('section', 'dp'), may hold values from 0.5 to 1.5
- out_weight: bfloat16 [2, 2048, 1024], P('section', 'dp'), may hold values from -0.125 to 0.125
Outputs:
- section_outputs: float32 [2, 2, 8192, 1024], P('section', None, 'dp')
- input_grads: float32 [2, 2, 8192, 1024], P('section', None, 'dp')
- grad_norm_gain: float32 [2, 1024], P('section', 'dp')
- grad_in_weight: float32 [2, 1024, 4384], P('section', 'dp')
- grad_conv_weight: float32 [2, 4, 2304], P('section', None, 'dp')
- grad_conv_bias: float32 [2, 2304], P('section', 'dp')
- grad_dt_bias: float32 [2, 32], P('section')
- grad_a_log: float32 [2, 32], P('section')
- grad_skip_gain: float32 [2, 32], P('section')
- grad_gate_gain: float32 [2, 2048], P('section', 'dp')
- grad_out_weight: float32 [2, 2048, 1024], P('section', 'dp')
The draws below stay inside these ranges and needn't reach their ends.
Inputs may be any that keep to these rules, and one draw needn't show every extreme that they name: `seq_lengths`: in each block the two lengths are at least 16 and sum to between 64 and 128; in each micro-batch some block is full, with lengths 128 - 16 and 16.
All inputs are finite; a program needn't handle non-finite values.
Results may differ from the reference program's by a relative error of at most 0.012.
Values may be sent and summed in bfloat16 or wider, within the bound.
No kernel may reach another device: no remote copies, remote signals or barrier semaphores. Data moves between devices by JAX's collectives and lax.ppermute only.
A program may use at most 256 MiB of HBM per device.

```python
import jax
import jax.numpy as jnp
from jax import lax

D = 1024
H = 32
P_SIZE = 64
N = 128
CONV = 4
MB = 2
TOK_DEV = 128
MIN_LEN = 16
DI = 2048
CH = 2304
PROJ = 4384
TOKENS = 8192
N_SECTION = 2


def draw_seq_lengths(key, part):
    key = jax.random.fold_in(key, 11)
    sub_keys = jax.random.split(key, 3)
    block_count = TOKENS // TOK_DEV
    filled = jax.random.randint(sub_keys[0], (MB, block_count), TOK_DEV // 2, TOK_DEV + 1)
    fullest = jax.random.randint(sub_keys[1], (MB, 1), 0, block_count)
    is_full = jnp.arange(block_count)[None, :] == fullest
    filled = jnp.where(is_full, TOK_DEV, filled)
    offsets = jax.random.randint(sub_keys[2], (MB, block_count), 0, TOK_DEV)
    leading = MIN_LEN + offsets % (filled - 2 * MIN_LEN + 1)
    leading = jnp.where(is_full, TOK_DEV - MIN_LEN, leading)
    trailing = filled - leading
    return jnp.stack([leading, trailing], axis=2).reshape(MB, 2 * block_count).astype(jnp.int32)


def levels(stream_key, dims, pieces, smallest, top_value):
    level, own = 1.0, jax.random.fold_in(stream_key, 6)
    for axis_at, parts in pieces:
        draws = jnp.exp(jax.random.uniform(jax.random.fold_in(own, axis_at), (parts,), jnp.float32, smallest / len(pieces), top_value / len(pieces)))
        level = level * jnp.repeat(draws, dims[axis_at] // parts).reshape([-1 if axis == axis_at else 1 for axis in range(len(dims))])
    return level


def scatter_about(rng, dims, deviation, limit, shards=(), kind=jnp.bfloat16):
    level = levels(rng, dims, shards, -0.22, 0.18) if shards else 1.0
    drawn = jax.random.normal(rng, dims, jnp.float32) * deviation * level
    return jnp.minimum(jnp.maximum(drawn, -limit), limit).astype(kind)


def setup_inputs(seed: int = 0) -> dict:
    seeds = jax.random.split(jax.random.key(seed), 13)
    return {
        "inputs": scatter_about(seeds[0], (MB, TOKENS, D), 1.0, 6.0, ((1, 64),)),
        "cotangent": scatter_about(seeds[1], (MB, TOKENS, D), 1.0, 6.0, ((1, 64),)),
        "seq_lengths": draw_seq_lengths(jax.random.fold_in(seeds[12], 71), 0),
        "norm_gain": jnp.clip(1.0 + 0.1 * jax.random.normal(seeds[3], (N_SECTION, D), jnp.float32), 0.5, 1.5).astype(jnp.bfloat16),
        "in_weight": scatter_about(seeds[4], (N_SECTION, D, PROJ), D ** -0.5, 0.1875, ((0, 2), (1, 64))),
        "conv_weight": scatter_about(seeds[5], (N_SECTION, CONV, CH), CONV ** -0.5, 3.0, ((0, 2), (2, 64))),
        "conv_bias": jnp.clip(jax.random.uniform(seeds[6], (N_SECTION, CH), jnp.float32, -0.5, 0.5) * levels(seeds[6], (N_SECTION, CH), ((0, 2), (1, 64)), -0.4, 0.0), -0.5, 0.5).astype(jnp.bfloat16),
        "dt_bias": jnp.clip(-6.0 + 4.0 * jax.random.uniform(seeds[7], (N_SECTION, H), jnp.float32) ** levels(seeds[7], (N_SECTION, H), ((0, 2),), -0.2, 0.2), -6.0, -2.0).astype(jnp.bfloat16),
        "a_log": jnp.clip(2.796875 * jax.random.uniform(seeds[8], (N_SECTION, H), jnp.float32) ** levels(seeds[8], (N_SECTION, H), ((0, 2),), -0.2, 0.2), 0.0, 2.796875).astype(jnp.bfloat16),
        "skip_gain": jnp.clip(0.5 + 1.0 * jax.random.uniform(seeds[9], (N_SECTION, H), jnp.float32) ** levels(seeds[9], (N_SECTION, H), ((0, 2),), -0.2, 0.2), 0.5, 1.5).astype(jnp.bfloat16),
        "gate_gain": jnp.clip(1.0 + 0.1 * jax.random.normal(seeds[10], (N_SECTION, DI), jnp.float32), 0.5, 1.5).astype(jnp.bfloat16),
        "out_weight": scatter_about(seeds[11], (N_SECTION, DI, D), DI ** -0.5, 0.125, ((0, 2), (1, 64))),
    }


@jax.custom_vjp
def low(v):
    return lax.optimization_barrier(v.astype(jnp.bfloat16)).astype(jnp.float32)

@jax.custom_vjp
def low_back(v):
    return v

def low_keep(v):
    return (low(v), None)

def low_pass(kept, grad):
    return (grad,)

def back_keep(v):
    return (v, None)

def back_low(kept, grad):
    return (low(grad),)
low.defvjp(low_keep, low_pass)
low_back.defvjp(back_keep, back_low)
EPS = 1e-05
PRECISE = lax.Precision.HIGHEST

def segment_layout(lengths, row_count):
    positions = jnp.arange(row_count, dtype=jnp.int32)
    boundary = lengths[0]
    filled = lengths[0] + lengths[1]
    segment = (positions >= boundary).astype(jnp.int32) + (positions >= filled).astype(jnp.int32)
    active = (positions < filled).astype(jnp.float32)
    return (segment, active)

def mixer(zx, conv_kernel, conv_shift, dt_shift, decay_param, skip_param, gate_param, segment):
    row_count = zx.shape[0]
    gate_part = zx[:, :DI]
    conv_in = zx[:, DI:DI + CH]
    dt_raw = zx[:, DI + CH:]
    conv_total = conv_shift[None, :] + conv_kernel[CONV - 1][None, :] * conv_in
    for lag_steps in range(1, CONV):
        shifted = jnp.concatenate([jnp.zeros((lag_steps, conv_in.shape[1]), conv_in.dtype), conv_in[:-lag_steps]], axis=0)
        shifted_seg = jnp.concatenate([jnp.full((lag_steps,), -1, jnp.int32), segment[:-lag_steps]])
        matching = (shifted_seg == segment).astype(conv_in.dtype)
        conv_total = conv_total + conv_kernel[CONV - 1 - lag_steps][None, :] * shifted * matching[:, None]
    conv_out = jax.nn.silu(conv_total)
    head_values = conv_out[:, :DI].reshape(row_count, H, P_SIZE)
    b_in = conv_out[:, DI:DI + N]
    c_out = conv_out[:, DI + N:]
    step_size = jax.nn.softplus(dt_raw + dt_shift[None, :])
    decay_rate = -jnp.exp(decay_param)
    decay_log = jnp.cumsum(step_size * decay_rate[None, :], axis=0)
    positions = jnp.arange(row_count)
    allowed = (positions[:, None] >= positions[None, :]) & (segment[:, None] == segment[None, :])
    log_gap = decay_log.T[:, :, None] - decay_log.T[:, None, :]
    decay_mat = jnp.where(allowed[None], jnp.exp(jnp.where(allowed[None], log_gap, 0.0)), 0.0)
    score_mat = jnp.dot(c_out, b_in.T, precision=PRECISE)
    mixing_mat = score_mat[None] * decay_mat * step_size.T[:, None, :]
    mixed_out = jnp.einsum('hij,jhp->ihp', mixing_mat, head_values, precision=PRECISE)
    mixed_out = mixed_out + skip_param[None, :, None] * head_values
    gated_out = mixed_out.reshape(row_count, DI) * jax.nn.silu(gate_part)
    norm_scale = lax.rsqrt(lax.optimization_barrier(jnp.mean(gated_out * gated_out, axis=1, keepdims=True)) + EPS)
    return gated_out * norm_scale * gate_param[None, :]

def layer(activation, lengths, params):
    norm_vec, w_in, conv_kernel, conv_shift, dt_shift, decay_param, skip_param, gate_param, w_out = params
    normed = activation * lax.rsqrt(lax.optimization_barrier(jnp.mean(activation * activation, axis=1, keepdims=True)) + EPS) * norm_vec[None, :]
    zx = low_back(jnp.dot(low(normed), w_in, precision=PRECISE))
    block_count = TOKENS // TOK_DEV
    blocks_zx = zx.reshape(block_count, TOK_DEV, PROJ)
    segments, actives = jax.vmap(lambda pair: segment_layout(pair, TOK_DEV))(lengths.reshape(block_count, 2))

    def one_block(block_item):
        block_rows, segment = block_item
        return mixer(block_rows, conv_kernel, conv_shift, dt_shift, decay_param, skip_param, gate_param, segment)
    normed_gate = lax.map(jax.checkpoint(one_block), (blocks_zx, segments)).reshape(TOKENS, DI)
    branch = low_back(jnp.dot(low(normed_gate), w_out, precision=PRECISE))
    return activation + actives.reshape(TOKENS)[:, None] * branch

def reference(inputs, cotangent, seq_lengths, norm_gain, in_weight, conv_weight, conv_bias, dt_bias, a_log, skip_gain, gate_gain, out_weight):
    weights = tuple((item.astype(jnp.float32) for item in (norm_gain, in_weight, conv_weight, conv_bias, dt_bias, a_log, skip_gain, gate_gain, out_weight)))
    start = inputs.astype(jnp.float32)
    probe = jnp.zeros_like(start)

    def forward(start, probe, weights):
        first_params = tuple((item[0] for item in weights))
        second_params = tuple((item[1] for item in weights))
        firsts = []
        finals = []
        for micro_index in range(MB):
            lengths = seq_lengths[micro_index]
            first_out = low(layer(start[micro_index], lengths, first_params))
            firsts.append(first_out)
            second_in = low_back(first_out + probe[micro_index])
            finals.append(layer(second_in, lengths, second_params))
        return (jnp.stack(finals), jnp.stack(firsts))
    finals, pull, firsts = jax.vjp(forward, start, probe, weights, has_aux=True)
    grad_start, grad_probe, grad_weights = pull(cotangent.astype(jnp.float32))
    section_outputs = jnp.stack([firsts, finals])
    input_grads = jnp.stack([grad_start, grad_probe])
    g_norm, g_in, g_conv, g_cbias, g_dt, g_alog, g_skip, g_gate, g_out = grad_weights
    return (section_outputs, input_grads, g_norm, g_in, g_conv, g_cbias, g_dt, g_alog, g_skip, g_gate, g_out)
```

```python
import jax
import jax.numpy as jnp
from jax import lax
from jax.sharding import PartitionSpec as P

H = 32
P_SIZE = 64
N = 128
CONV = 4
DI = 2048
CH = 2304


EPS = 1e-05
PRECISE = lax.Precision.HIGHEST


def shifted_2(block, axis, distance):
    devices = range(lax.axis_size(axis))
    route = [(i - distance, i) for i in devices if i - distance in devices]
    return lax.ppermute(block, axis, route)


def segment_layout(lengths, row_count):
    positions = jnp.arange(row_count, dtype=jnp.int32)
    boundary = lengths[0]
    filled = lengths[0] + lengths[1]
    segment = (positions >= boundary).astype(jnp.int32) + (positions >= filled).astype(jnp.int32)
    active = (positions < filled).astype(jnp.float32)
    return (segment, active)


def mixer(zx, conv_kernel, conv_shift, dt_shift, decay_param, skip_param, gate_param, segment):
    row_count = zx.shape[0]
    gate_part = zx[:, :DI]
    conv_in = zx[:, DI : DI + CH]
    dt_raw = zx[:, DI + CH :]
    conv_total = conv_shift[None, :] + conv_kernel[CONV - 1][None, :] * conv_in
    for lag_steps in range(1, CONV):
        shifted = jnp.concatenate(
            [jnp.zeros((lag_steps, conv_in.shape[1]), conv_in.dtype), conv_in[:-lag_steps]], axis=0
        )
        shifted_seg = jnp.concatenate([jnp.full((lag_steps,), -1, jnp.int32), segment[:-lag_steps]])
        matching = (shifted_seg == segment).astype(conv_in.dtype)
        conv_total = (
            conv_total + conv_kernel[CONV - 1 - lag_steps][None, :] * shifted * matching[:, None]
        )
    conv_out = jax.nn.silu(conv_total)
    head_values = conv_out[:, :DI].reshape(row_count, H, P_SIZE)
    b_in = conv_out[:, DI : DI + N]
    c_out = conv_out[:, DI + N :]
    step_size = jax.nn.softplus(dt_raw + dt_shift[None, :])
    decay_rate = -jnp.exp(decay_param)
    decay_log = jnp.cumsum(step_size * decay_rate[None, :], axis=0)
    positions = jnp.arange(row_count)
    allowed = (positions[:, None] >= positions[None, :]) & (segment[:, None] == segment[None, :])
    log_gap = decay_log.T[:, :, None] - decay_log.T[:, None, :]
    decay_mat = jnp.where(allowed[None], jnp.exp(jnp.where(allowed[None], log_gap, 0.0)), 0.0)
    score_mat = jnp.dot(c_out, b_in.T, precision=PRECISE)
    mixing_mat = score_mat[None] * decay_mat * step_size.T[:, None, :]
    mixed_out = jnp.einsum("hij,jhp->ihp", mixing_mat, head_values, precision=PRECISE)
    mixed_out = mixed_out + skip_param[None, :, None] * head_values
    gated_out = mixed_out.reshape(row_count, DI) * jax.nn.silu(gate_part)
    norm_scale = lax.rsqrt(jnp.mean(gated_out * gated_out, axis=1, keepdims=True) + EPS)
    return gated_out * norm_scale * gate_param[None, :]


def rms_norm(activation, gain_vec):
    return (
        activation
        * lax.rsqrt(jnp.mean(activation * activation, axis=1, keepdims=True) + EPS)
        * gain_vec[None, :]
    )


def layer_forward(activation, lengths, weights, head_params):
    w_in, w_out, norm_vec, conv_kernel, conv_shift, gate_param = weights
    normed = rms_norm(activation, norm_vec.astype(jnp.float32))
    zx = jnp.dot(normed.astype(jnp.bfloat16), w_in, preferred_element_type=jnp.float32)
    segment, active = segment_layout(lengths, activation.shape[0])
    normed_gate = mixer(
        zx,
        conv_kernel.astype(jnp.float32),
        conv_shift.astype(jnp.float32),
        head_params[0],
        head_params[1],
        head_params[2],
        gate_param.astype(jnp.float32),
        segment,
    )
    branch = jnp.dot(normed_gate.astype(jnp.bfloat16), w_out, preferred_element_type=jnp.float32)
    return activation + active[:, None] * branch


def layer_backward(activation, grad_out, lengths, weights, head_params):
    w_in, w_out, norm_vec, conv_kernel, conv_shift, gate_param = weights
    normed, norm_pull = jax.vjp(rms_norm, activation, norm_vec.astype(jnp.float32))
    normed_low = normed.astype(jnp.bfloat16)
    zx = jnp.dot(normed_low, w_in, preferred_element_type=jnp.float32)
    segment, active = segment_layout(lengths, activation.shape[0])

    def local_mixer(zx_in, kernel_in, shift_in, dt_in, decay_in, skip_in, gate_in):
        return mixer(zx_in, kernel_in, shift_in, dt_in, decay_in, skip_in, gate_in, segment)

    normed_gate, mixer_pull = jax.vjp(
        local_mixer,
        zx,
        conv_kernel.astype(jnp.float32),
        conv_shift.astype(jnp.float32),
        head_params[0],
        head_params[1],
        head_params[2],
        gate_param.astype(jnp.float32),
    )
    gate_low = normed_gate.astype(jnp.bfloat16)
    grad_branch = (active[:, None] * grad_out).astype(jnp.bfloat16)
    grad_w_out = jnp.einsum("tf,td->fd", gate_low, grad_branch, preferred_element_type=jnp.float32)
    grad_gate = jnp.einsum("td,fd->tf", grad_branch, w_out, preferred_element_type=jnp.float32)
    pulled = mixer_pull(grad_gate)
    grad_zx = pulled[0].astype(jnp.bfloat16)
    grad_w_in = jnp.einsum("td,tf->df", normed_low, grad_zx, preferred_element_type=jnp.float32)
    grad_normed = jnp.einsum("tf,df->td", grad_zx, w_in, preferred_element_type=jnp.float32)
    grad_act, grad_norm_vec = norm_pull(grad_normed)
    weight_terms = (grad_w_in, grad_w_out, grad_norm_vec, pulled[1], pulled[2], pulled[6])
    head_terms = (pulled[3], pulled[4], pulled[5])
    return (grad_out + grad_act, weight_terms, head_terms)


def add_terms(left_terms, right_terms):
    return tuple((left_item + right_item for left_item, right_item in zip(left_terms, right_terms)))


def masked_terms(terms, weight_flag):
    return tuple(
        (jnp.where(weight_flag, term_item, jnp.zeros_like(term_item)) for term_item in terms)
    )


SMALL = 16
WIDE = 4480


def split_small(flat, n):
    cuts = [0, 1024 // n, 1024 // n + 4 * CH // n, 1024 // n + 5 * CH // n, 1024 // n + 5 * CH // n + DI // n]
    parts = [flat[:, a:b] for a, b in zip(cuts[:-1], cuts[1:])]
    conv = parts[1].reshape(n, CONV, CH // n).transpose(1, 0, 2).reshape(CONV, CH)
    return parts[0].reshape(-1), conv, parts[2].reshape(-1), parts[3].reshape(-1)


def join_small(norm, conv, bias, gate, n):
    conv_rows = conv.reshape(CONV, n, CH // n).transpose(1, 0, 2).reshape(n, -1)
    return jnp.concatenate([norm.reshape(n, -1), conv_rows, bias.reshape(n, -1), gate.reshape(n, -1)], axis=1)


def gather_weights(in_shard, out_shard, norm, conv, bias, gate):
    rows = in_shard.shape[0]
    n = lax.axis_size("dp")
    small = jnp.concatenate([norm, conv.reshape(-1), bias, gate])
    small = jnp.pad(small, (0, rows * SMALL - small.shape[0])).reshape(rows, SMALL)
    zeros = jnp.zeros((rows, WIDE - in_shard.shape[1] - SMALL), in_shard.dtype)
    pack = jnp.concatenate([in_shard, small, zeros, out_shard[:rows], out_shard[rows:]], axis=1)
    whole = lax.all_gather(pack, "dp", axis=0, tiled=False)
    proj = in_shard.shape[1]
    flat = whole[:, :, proj : proj + SMALL].reshape(n, rows * SMALL)
    norm_all, conv_all, bias_all, gate_all = split_small(flat, n)
    w_in = whole[:, :, :proj].reshape(n * rows, proj)
    out_lo = whole[:, :, WIDE : WIDE + 1024]
    out_hi = whole[:, :, WIDE + 1024 :]
    w_out = jnp.concatenate([out_lo, out_hi], axis=1).reshape(2 * n * rows, 1024)
    return (w_in, w_out, norm_all, conv_all, bias_all, gate_all)


def high_low(values):
    high = values.astype(jnp.bfloat16)
    return high, (values - high.astype(jnp.float32)).astype(jnp.bfloat16)


def reduce_grads(weight_sums, head_sums):
    n = lax.axis_size("dp")
    w_in, w_out, norm, conv, bias, gate = weight_sums
    rows, proj = w_in.shape[0] // n, w_in.shape[1]
    heads = jnp.concatenate(head_sums)
    small = join_small(norm, conv, bias, gate, n)
    small = jnp.pad(small, ((0, 0), (0, rows * SMALL - small.shape[1])))
    heads_each = jnp.broadcast_to(heads[None], (n, heads.shape[0]))
    heads_each = jnp.pad(heads_each, ((0, 0), (0, rows * SMALL - heads.shape[0])))
    extra = [item.reshape(n, rows, SMALL) for item in (*high_low(small), *high_low(heads_each))]
    zeros = jnp.zeros((n, rows, WIDE - proj - 4 * SMALL), jnp.bfloat16)
    send_in = jnp.concatenate([w_in.astype(jnp.bfloat16).reshape(n, rows, proj), *extra, zeros], axis=2)
    send_out = w_out.astype(jnp.bfloat16).reshape(n, 2 * rows, 1024)
    got_out = lax.all_to_all(send_out, "dp", 0, 0)
    got_in = lax.all_to_all(send_in, "dp", 0, 0)
    sum_in = jnp.sum(got_in.astype(jnp.float32), axis=0)
    sum_out = jnp.sum(got_out.astype(jnp.float32), axis=0)
    own = [sum_in[:, proj + i * SMALL : proj + (i + 1) * SMALL].reshape(-1) for i in range(4)]
    flat, heads = own[0] + own[1], (own[2] + own[3])[: heads.shape[0]]
    cuts = [0, 1024 // n, 1024 // n + 4 * CH // n, 1024 // n + 5 * CH // n, 1024 // n + 5 * CH // n + DI // n]
    parts = [flat[a:b] for a, b in zip(cuts[:-1], cuts[1:])]
    return (
        (sum_in[:, :proj], sum_out, parts[0], parts[1].reshape(CONV, -1), parts[2], parts[3]),
        (heads[:H], heads[H : 2 * H], heads[2 * H :]),
    )


def body(
    inputs,
    cotangent,
    seq_lengths,
    norm_gain,
    in_weight,
    conv_weight,
    conv_bias,
    dt_bias,
    a_log,
    skip_gain,
    gate_gain,
    out_weight,
):
    section_index = lax.axis_index("section")
    micro_count = inputs.shape[0]
    row_count = inputs.shape[1]
    width = inputs.shape[2]
    shards = (in_weight[0], out_weight[0], norm_gain[0], conv_weight[0], conv_bias[0], gate_gain[0])
    gathered = gather_weights(*shards)
    head_params = (
        dt_bias[0].astype(jnp.float32),
        a_log[0].astype(jnp.float32),
        skip_gain[0].astype(jnp.float32),
    )
    kept_inputs = []
    outputs_by_step = []
    received = jnp.zeros((row_count, width), jnp.float32)
    for step_index in range(micro_count + 1):
        own_rows = inputs[min(step_index, micro_count - 1)].astype(jnp.float32)
        current = jnp.where(section_index == 0, own_rows, received)
        micro_pick = jnp.clip(step_index - section_index, 0, micro_count - 1)
        lengths = lax.dynamic_index_in_dim(seq_lengths, micro_pick, 0, keepdims=False)
        result = layer_forward(current, lengths, gathered, head_params)
        outgoing = result.astype(jnp.bfloat16)
        kept_inputs.append(current)
        outputs_by_step.append(jnp.where(section_index == 0, outgoing.astype(jnp.float32), result))
        if step_index < micro_count:
            received = shifted_2(outgoing, "section", 1).astype(jnp.float32)
    section_outputs = jnp.stack(
        [
            jnp.where(
                section_index == 0, outputs_by_step[micro_index], outputs_by_step[micro_index + 1]
            )
            for micro_index in range(micro_count)
        ]
    )
    backward_weights = gathered
    stacked_inputs = jnp.stack(kept_inputs)
    weight_sums = None
    head_sums = None
    grads_by_step = []
    incoming = jnp.zeros((row_count, width), jnp.float32)
    for step_index in range(micro_count + 1):
        own_grad = cotangent[min(step_index, micro_count - 1)].astype(jnp.float32)
        grad_out = jnp.where(section_index == 1, own_grad, incoming)
        micro_place = step_index - 1 + section_index
        micro_pick = jnp.clip(micro_place, 0, micro_count - 1)
        in_range = (micro_place >= 0) & (micro_place < micro_count)
        current = lax.dynamic_index_in_dim(
            stacked_inputs, micro_pick + section_index, 0, keepdims=False
        )
        lengths = lax.dynamic_index_in_dim(seq_lengths, micro_pick, 0, keepdims=False)
        grad_input, weight_terms, head_terms = layer_backward(
            current, grad_out, lengths, backward_weights, head_params
        )
        weight_terms = masked_terms(weight_terms, in_range)
        head_terms = masked_terms(head_terms, in_range)
        if weight_sums is None:
            weight_sums = weight_terms
            head_sums = head_terms
        else:
            weight_sums = add_terms(weight_sums, weight_terms)
            head_sums = add_terms(head_sums, head_terms)
        outgoing = grad_input.astype(jnp.bfloat16)
        grads_by_step.append(
            jnp.where(section_index == 0, grad_input, outgoing.astype(jnp.float32))
        )
        if step_index < micro_count:
            incoming = shifted_2(outgoing, "section", -1).astype(jnp.float32)
    input_grads = jnp.stack(
        [
            jnp.where(
                section_index == 0, grads_by_step[micro_index + 1], grads_by_step[micro_index]
            )
            for micro_index in range(micro_count)
        ]
    )
    (grad_w_in, grad_w_out, grad_norm_vec, grad_kernel, grad_shift, grad_gate_vec), (
        grad_dt,
        grad_decay,
        grad_skip,
    ) = reduce_grads(weight_sums, head_sums)
    return (
        section_outputs[None],
        input_grads[None],
        grad_norm_vec[None],
        grad_w_in[None],
        grad_kernel[None],
        grad_shift[None],
        grad_dt[None],
        grad_decay[None],
        grad_skip[None],
        grad_gate_vec[None],
        grad_w_out[None],
    )


def solution(mesh):
    in_specs = (
        P(None, "dp", None),
        P(None, "dp", None),
        P(None, "dp"),
        P("section", "dp"),
        P("section", "dp", None),
        P("section", None, "dp"),
        P("section", "dp"),
        P("section", None),
        P("section", None),
        P("section", None),
        P("section", "dp"),
        P("section", "dp", None),
    )
    out_specs = (
        P("section", None, "dp", None),
        P("section", None, "dp", None),
        P("section", "dp"),
        P("section", "dp", None),
        P("section", None, "dp"),
        P("section", "dp"),
        P("section", None),
        P("section", None),
        P("section", None),
        P("section", "dp"),
        P("section", "dp", None),
    )
    return jax.shard_map(body, mesh=mesh, in_specs=in_specs, out_specs=out_specs, check_vma=False)
```

```python
import functools

import jax
import jax.numpy as jnp
from jax import lax
from jax.experimental import pallas as pl
from jax.experimental.pallas import tpu as pltpu
from jax.sharding import PartitionSpec as P

H = 32
CONV = 4
D = 1024
DI = 2048
CH = 2304
PROJ = 4384
ROWS = 128
SMALL = 16
WIDE = 4480
PACK = WIDE + 2 * D
EPS = 1e-05
PRECISE = lax.Precision.HIGHEST
F32 = jnp.float32
BF16 = jnp.bfloat16
VMEM_LIMIT = 50 * 1024 * 1024


def pass_section(block, distance):
    devices = range(lax.axis_size("section"))
    route = [(i - distance, i) for i in devices if i - distance in devices]
    return lax.ppermute(block, "section", route)


def dot_nt(left, right, precision=None):
    return lax.dot_general(
        left, right, (((1,), (1,)), ((), ())), precision=precision, preferred_element_type=F32
    )


def dot_tn(left, right, precision=None):
    return lax.dot_general(
        left, right, (((0,), (0,)), ((), ())), precision=precision, preferred_element_type=F32
    )


def column_iota(shape, axis):
    return lax.broadcasted_iota(jnp.int32, shape, axis)


def lag_masks(first, filled):
    at = column_iota((ROWS, 1), 0)
    own = (at >= first).astype(jnp.int32) + (at >= filled).astype(jnp.int32)
    masks = []
    for lag in range(1, CONV):
        earlier = (at - lag >= first).astype(jnp.int32) + (at - lag >= filled).astype(jnp.int32)
        masks.append(((at >= lag) & (earlier == own)).astype(F32))
    return masks


def pair_mask(first, filled):
    i = column_iota((ROWS, ROWS), 0)
    j = column_iota((ROWS, ROWS), 1)
    seg_i = (i >= first).astype(jnp.int32) + (i >= filled).astype(jnp.int32)
    seg_j = (j >= first).astype(jnp.int32) + (j >= filled).astype(jnp.int32)
    return (i >= j) & (seg_i == seg_j)


IN_CHUNKS = tuple((start, 512) for start in range(0, 4096, 512)) + ((4096, 384),)


def layer_kernel(
    with_back,
    lens_ref,
    v_ref,
    dout_ref,
    norm_ref,
    taps_ref,
    bias_ref,
    dtb_ref,
    rate_ref,
    skip_ref,
    gate_ref,
    pack_ref,
    *rest,
):
    if with_back:
        (out_ref, outb_ref, dv_ref, dvb_ref, nb_ref, gn_ref, gb_ref, dzx_ref) = rest[:8]
        (dnorm_ref, dtaps_ref, dbias_ref, dgate_ref, dskip_ref, ddtb_ref, drate_ref) = rest[8:15]
        rest = rest[15:]
    else:
        (outb_ref, nb_ref, gn_ref) = rest[:3]
        rest = rest[3:]
    (win, wout, sems, zx, xc, slope, decay, ys, gs, cum_t, dt_t) = rest[:11]
    blocks = win.shape[0]
    quarter = blocks // 4
    block_rows = win.shape[1]

    copies = [
        pltpu.make_async_copy(
            pack_ref.at[:, :, pl.ds(start, size)], win.at[:, :, pl.ds(start, size)], sems.at[k]
        )
        for k, (start, size) in enumerate(IN_CHUNKS)
    ]
    for half in range(2):
        copies.append(
            pltpu.make_async_copy(
                pack_ref.at[:, :, pl.ds(WIDE + half * D, D)],
                wout.at[:, pl.ds(half * block_rows, block_rows), :],
                sems.at[len(IN_CHUNKS) + half],
            )
        )
    for copy in copies:
        copy.start()

    first = lens_ref[0]
    filled = lens_ref[0] + lens_ref[1]
    masks = lag_masks(first, filled)
    active = (column_iota((ROWS, 1), 0) < filled).astype(F32)
    lane = column_iota((ROWS, ROWS), 1)
    low_lanes = lane < 64
    head_lanes = lane < H

    v = v_ref[...].astype(F32)
    r = lax.rsqrt(jnp.mean(v * v, axis=1, keepdims=True) + EPS)
    nb_ref[...] = (v * r * norm_ref[...]).astype(BF16)

    for k, (start, size) in enumerate(IN_CHUNKS):
        copies[k].wait()
        zx[:, pl.ds(start, size)] = jnp.dot(
            nb_ref[...],
            win[:, :, pl.ds(start, size)].reshape(D, size),
            preferred_element_type=F32,
        )

    def conv_step(c, carry):
        at = pl.ds(pl.multiple_of(c * 256, 256), 256)
        u = zx[:, pl.ds(pl.multiple_of(DI + c * 256, 256), 256)]
        taps = taps_ref[:, at]
        total = bias_ref[:, at] + taps[CONV - 1 : CONV] * u
        for lag in range(1, CONV):
            total += taps[CONV - 1 - lag : CONV - lag] * (pltpu.roll(u, lag, 0) * masks[lag - 1])
        sig = jax.nn.sigmoid(total)
        xc[:, at] = total * sig
        if with_back:
            slope[:, at] = sig * (1.0 + total * (1.0 - sig))
        return carry

    lax.fori_loop(0, CH // 256, conv_step, 0)

    raw = jnp.where(head_lanes, zx[:, DI + CH :], 0.0) + dtb_ref[...]
    dt = jnp.maximum(raw, 0.0) + jnp.log1p(jnp.exp(-jnp.abs(raw)))
    dt = jnp.where(head_lanes, dt, 0.0)
    rate = rate_ref[...]
    lower = (column_iota((ROWS, ROWS), 0) >= lane).astype(F32)
    cum = jnp.dot(lower, dt * rate, precision=PRECISE, preferred_element_type=F32)
    cum_t[...] = cum.T
    dt_t[...] = dt.T
    allowed = pair_mask(first, filled)
    bb = xc[:, DI : DI + 128]
    cc = xc[:, DI + 128 :]
    score = dot_nt(cc, bb, PRECISE)

    def head_group(g, carry):
        turned = pltpu.roll(cum, lax.rem(ROWS - 8 * g, ROWS), 1)
        rows = pl.ds(pl.multiple_of(g * 8, 8), 8)
        cum_rows = cum_t[rows, :]
        dt_rows = dt_t[rows, :]
        for pair in range(4):
            at = pl.ds(pl.multiple_of(g * 512 + pair * 128, 128), 128)
            mixes = []
            for k in (2 * pair, 2 * pair + 1):
                gap = turned[:, k : k + 1] - cum_rows[k : k + 1, :]
                fade = jnp.exp(jnp.where(allowed, gap, -1e30))
                if with_back:
                    decay[g * 8 + k] = fade
                mixes.append((score * fade * dt_rows[k : k + 1, :]).astype(BF16))
            x = xc[:, at]
            halves = [jnp.where(low_lanes, x, 0.0), jnp.where(low_lanes, 0.0, x)]
            ys[:, at] = (
                jnp.dot(
                    jnp.concatenate(mixes, axis=1),
                    jnp.concatenate(halves, axis=0).astype(BF16),
                    preferred_element_type=F32,
                )
                + skip_ref[:, at] * x
            )
        return carry

    lax.fori_loop(0, H // 8, head_group, 0)

    def gate_step(c, total):
        at = pl.ds(pl.multiple_of(c * 256, 256), 256)
        z = zx[:, at]
        g = ys[:, at] * (z * jax.nn.sigmoid(z))
        gs[:, at] = g
        return total + jnp.sum(g * g, axis=1, keepdims=True)

    total = lax.fori_loop(0, DI // 256, gate_step, jnp.zeros((ROWS, 1), F32))
    q = lax.rsqrt(total * (1.0 / DI) + EPS)

    def gain_step(c, carry):
        at = pl.ds(pl.multiple_of(c * 256, 256), 256)
        gn_ref[:, at] = (gs[:, at] * q * gate_ref[:, at]).astype(BF16)
        return carry

    lax.fori_loop(0, DI // 256, gain_step, 0)

    for copy in copies[len(IN_CHUNKS) :]:
        copy.wait()

    def branch_step(c, carry):
        at = pl.ds(pl.multiple_of(c * 512, 512), 512)
        branch = jnp.dot(
            gn_ref[...], wout[:, :, at].reshape(DI, 512), preferred_element_type=F32
        )
        result = v_ref[:, at].astype(F32) + active * branch
        outb_ref[:, at] = result.astype(BF16)
        if with_back:
            out_ref[:, at] = result
        return carry

    lax.fori_loop(0, D // 512, branch_step, 0)
    if not with_back:
        return

    (dgs, dxc, row_part, col_part, dscore) = rest[11:]
    gb_ref[...] = (active * dout_ref[...].astype(F32)).astype(BF16)

    def dgate_step(c, total):
        at = pl.ds(pl.multiple_of(c * 512, 512), 512)
        weight = wout[pl.ds(c * quarter, quarter)].reshape(512, D)
        dgn = dot_nt(gb_ref[...], weight)
        g = gs[:, at]
        dgate_ref[:, at] = jnp.sum(dgn * (g * q), axis=0, keepdims=True)
        pulled = dgn * gate_ref[:, at]
        dgs[:, at] = pulled
        return total + jnp.sum(pulled * g, axis=1, keepdims=True)

    total = lax.fori_loop(0, 4, dgate_step, jnp.zeros((ROWS, 1), F32))
    pull = q * q * q * (total * (1.0 / DI))

    def dz_step(c, carry):
        at = pl.ds(pl.multiple_of(c * 256, 256), 256)
        dg = q * dgs[:, at] - gs[:, at] * pull
        z = zx[:, at]
        sig = jax.nn.sigmoid(z)
        dy = dg * (z * sig)
        dgs[:, at] = dy
        dzx_ref[:, at] = (dg * ys[:, at] * (sig * (1.0 + z * (1.0 - sig)))).astype(BF16)
        dskip_ref[:, at] = jnp.sum(dy * xc[:, at], axis=0, keepdims=True)
        return carry

    lax.fori_loop(0, DI // 256, dz_step, 0)

    row_part[...] = jnp.zeros((ROWS, ROWS), F32)
    col_part[...] = jnp.zeros((ROWS, ROWS), F32)
    dscore[...] = jnp.zeros((ROWS, ROWS), F32)

    def head_back(g, carry):
        rows = pl.ds(pl.multiple_of(g * 8, 8), 8)
        dt_rows = dt_t[rows, :]
        col_sums = []
        row_sum = row_part[...]
        dscore_sum = dscore[...]
        for pair in range(4):
            at = pl.ds(pl.multiple_of(g * 512 + pair * 128, 128), 128)
            dy = dgs[:, at]
            dys = jnp.concatenate(
                [jnp.where(low_lanes, dy, 0.0), jnp.where(low_lanes, 0.0, dy)], axis=0
            ).astype(BF16)
            dmix = dot_nt(dys, xc[:, at].astype(BF16))
            mixes = []
            for side in range(2):
                k = 2 * pair + side
                dt_row = dt_rows[k : k + 1, :]
                fade = decay[g * 8 + k]
                part = dmix[side * ROWS : (side + 1) * ROWS] * fade
                dscore_sum += part * dt_row
                part = part * score
                col_sums.append(jnp.sum(part, axis=0, keepdims=True))
                row_sum += jnp.where(
                    lane == g * 8 + k, jnp.sum(part * dt_row, axis=1, keepdims=True), 0.0
                )
                mixes.append((score * fade * dt_row).astype(BF16))
            dxc[:, at] = dot_tn(jnp.concatenate(mixes, axis=0), dys) + skip_ref[:, at] * dy
        col_part[rows, :] = jnp.concatenate(col_sums, axis=0)
        row_part[...] = row_sum
        dscore[...] = dscore_sum
        return carry

    lax.fori_loop(0, H // 8, head_back, 0)

    col_sum = col_part[...].T
    dcum = row_part[...] - dt * col_sum
    dlog = dot_tn(lower, dcum, PRECISE)
    drate_ref[...] = jnp.sum(dlog * dt, axis=0, keepdims=True) * rate
    draw = jnp.where(head_lanes, (col_sum + dlog * rate) * jax.nn.sigmoid(raw), 0.0)
    ddtb_ref[...] = jnp.sum(draw, axis=0, keepdims=True)
    dzx_ref[:, DI + CH :] = draw.astype(BF16)
    dxc[:, DI : DI + 128] = dot_tn(dscore[...], cc, PRECISE)
    dxc[:, DI + 128 :] = jnp.dot(dscore[...], bb, precision=PRECISE, preferred_element_type=F32)

    def dconv_step(c, carry):
        at = pl.ds(pl.multiple_of(c * 256, 256), 256)
        wide_at = pl.ds(pl.multiple_of(DI + c * 256, 256), 256)
        u = zx[:, wide_at]
        taps = taps_ref[:, at]
        dconv = dxc[:, at] * slope[:, at]
        dbias_ref[:, at] = jnp.sum(dconv, axis=0, keepdims=True)
        du = taps[CONV - 1 : CONV] * dconv
        dtaps_ref[CONV - 1 : CONV, at] = jnp.sum(dconv * u, axis=0, keepdims=True)
        for lag in range(1, CONV):
            masked = dconv * masks[lag - 1]
            k = CONV - 1 - lag
            dtaps_ref[k : k + 1, at] = jnp.sum(
                masked * pltpu.roll(u, lag, 0), axis=0, keepdims=True
            )
            du += taps[k : k + 1] * pltpu.roll(masked, ROWS - lag, 0)
        dzx_ref[:, wide_at] = du.astype(BF16)
        return carry

    lax.fori_loop(0, CH // 256, dconv_step, 0)

    def dnorm_step(c, total):
        at = pl.ds(pl.multiple_of(c * 256, 256), 256)
        weight = win[pl.ds(c * quarter, quarter)].reshape(256, WIDE)
        dnormed = dot_nt(dzx_ref[...], weight)
        vc = v_ref[:, at].astype(F32)
        dnorm_ref[:, at] = jnp.sum(dnormed * (vc * r), axis=0, keepdims=True)
        pulled = dnormed * norm_ref[:, at]
        dv_ref[:, at] = pulled
        return total + jnp.sum(pulled * vc, axis=1, keepdims=True)

    total = lax.fori_loop(0, 4, dnorm_step, jnp.zeros((ROWS, 1), F32))
    pull = r * r * r * (total * (1.0 / D))

    def dv_step(c, carry):
        at = pl.ds(pl.multiple_of(c * 256, 256), 256)
        result = (
            dout_ref[:, at].astype(F32) + r * dv_ref[:, at] - v_ref[:, at].astype(F32) * pull
        )
        dv_ref[:, at] = result
        dvb_ref[:, at] = result.astype(BF16)
        return carry

    lax.fori_loop(0, D // 256, dv_step, 0)


def run_layer(with_back, lens, v, dout, params, pack):
    blocks, block_rows = pack.shape[0], pack.shape[1]
    vmem = pl.BlockSpec(memory_space=pltpu.VMEM)
    shape = jax.ShapeDtypeStruct
    if with_back:
        outs = [
            shape((ROWS, D), F32),
            shape((ROWS, D), BF16),
            shape((ROWS, D), F32),
            shape((ROWS, D), BF16),
            shape((ROWS, D), BF16),
            shape((ROWS, DI), BF16),
            shape((ROWS, D), BF16),
            shape((ROWS, WIDE), BF16),
            shape((1, D), F32),
            shape((CONV, CH), F32),
            shape((1, CH), F32),
            shape((1, DI), F32),
            shape((1, DI), F32),
            shape((1, ROWS), F32),
            shape((1, ROWS), F32),
        ]
    else:
        outs = [shape((ROWS, D), BF16), shape((ROWS, D), BF16), shape((ROWS, DI), BF16)]
    scratch = [
        pltpu.VMEM((blocks, block_rows, WIDE), BF16),
        pltpu.VMEM((blocks, 2 * block_rows, D), BF16),
        pltpu.SemaphoreType.DMA((len(IN_CHUNKS) + 2,)),
        pltpu.VMEM((ROWS, WIDE), F32),
        pltpu.VMEM((ROWS, CH), F32),
        pltpu.VMEM((ROWS, CH), F32),
        pltpu.VMEM((H, ROWS, ROWS), F32),
        pltpu.VMEM((ROWS, DI), F32),
        pltpu.VMEM((ROWS, DI), F32),
        pltpu.VMEM((ROWS, ROWS), F32),
        pltpu.VMEM((ROWS, ROWS), F32),
    ]
    if with_back:
        scratch += [
            pltpu.VMEM((ROWS, DI), F32),
            pltpu.VMEM((ROWS, CH), F32),
            pltpu.VMEM((ROWS, ROWS), F32),
            pltpu.VMEM((ROWS, ROWS), F32),
            pltpu.VMEM((ROWS, ROWS), F32),
        ]
    flops = 2 * ROWS * (WIDE * D + DI * D) * (2 if with_back else 1)
    return pl.pallas_call(
        functools.partial(layer_kernel, with_back),
        out_shape=outs,
        in_specs=[pl.BlockSpec(memory_space=pltpu.SMEM)]
        + [vmem] * 9
        + [pl.BlockSpec(memory_space=pl.ANY)],
        out_specs=[vmem] * len(outs),
        scratch_shapes=scratch,
        cost_estimate=pl.CostEstimate(
            flops=flops, bytes_accessed=D * PACK * 2, transcendentals=H * ROWS * ROWS
        ),
        compiler_params=pltpu.CompilerParams(vmem_limit_bytes=VMEM_LIMIT),
        name="layer_both" if with_back else "layer_forward",
    )(lens, v, dout, *params, pack)


GRAD_CHUNK = 640


def in_grad_kernel(first_ref, second_ref, dzx_ref, dzx2_ref, extra_ref, out_ref, turned):
    step = pl.program_id(0)

    @pl.when(step == 0)
    def _():
        turned[:, :ROWS] = first_ref[...].T
        turned[:, ROWS:] = second_ref[...].T

    both = jnp.concatenate([dzx_ref[...], dzx2_ref[...]], axis=0)
    grad = jnp.dot(turned[...], both, preferred_element_type=F32).astype(BF16)
    out_ref[...] = grad.reshape(out_ref.shape)

    @pl.when(step == WIDE // GRAD_CHUNK - 1)
    def _():
        last = pl.ds(GRAD_CHUNK - 128, 128)
        spare = lax.broadcasted_iota(jnp.int32, extra_ref.shape, 2) >= PROJ - WIDE + 128
        kept = out_ref[:, :, last].astype(F32)
        out_ref[:, :, last] = jnp.where(spare, extra_ref[...].astype(F32), kept).astype(BF16)


def in_grad(first, second, dzx, dzx2, extra):
    blocks, block_rows = extra.shape[0], extra.shape[1]
    return pl.pallas_call(
        in_grad_kernel,
        grid=(WIDE // GRAD_CHUNK,),
        out_shape=jax.ShapeDtypeStruct((blocks, block_rows, WIDE), BF16),
        in_specs=[
            pl.BlockSpec((ROWS, D), lambda i: (0, 0)),
            pl.BlockSpec((ROWS, D), lambda i: (0, 0)),
            pl.BlockSpec((ROWS, GRAD_CHUNK), lambda i: (0, i)),
            pl.BlockSpec((ROWS, GRAD_CHUNK), lambda i: (0, i)),
            pl.BlockSpec((blocks, block_rows, 128), lambda i: (0, 0, 0)),
        ],
        out_specs=pl.BlockSpec((blocks, block_rows, GRAD_CHUNK), lambda i: (0, 0, i)),
        scratch_shapes=[pltpu.VMEM((D, 2 * ROWS), BF16)],
        cost_estimate=pl.CostEstimate(
            flops=4 * ROWS * D * WIDE, bytes_accessed=D * WIDE * 2, transcendentals=0
        ),
        compiler_params=pltpu.CompilerParams(vmem_limit_bytes=VMEM_LIMIT),
        name="in_weight_grad",
    )(first, second, dzx, dzx2, extra)


def small_cuts(n):
    cuts = [0]
    for size in (D, CONV * CH, CH, DI):
        cuts.append(cuts[-1] + size // n)
    return list(zip(cuts[:-1], cuts[1:]))


def gather_weights(in_shard, out_shard, norm, conv, bias, gate):
    rows = in_shard.shape[0]
    n = lax.axis_size("dp")
    small = jnp.concatenate([norm, conv.reshape(-1), bias, gate])
    small = jnp.pad(small, (0, rows * SMALL - small.shape[0])).reshape(rows, SMALL)
    zeros = jnp.zeros((rows, WIDE - PROJ - SMALL), BF16)
    pack = jnp.concatenate([in_shard, small, zeros, out_shard[:rows], out_shard[rows:]], axis=1)
    whole = lax.all_gather(pack, "dp", axis=0, tiled=False)
    flat = whole[:, :, PROJ : PROJ + SMALL].reshape(n, rows * SMALL).astype(F32)
    norm_all, conv_all, bias_all, gate_all = [flat[:, a:b] for a, b in small_cuts(n)]
    conv_all = conv_all.reshape(n, CONV, CH // n).transpose(1, 0, 2).reshape(CONV, CH)
    return (whole, norm_all.reshape(1, D), conv_all, bias_all.reshape(1, CH), gate_all.reshape(1, DI))


def high_low(values):
    high = values.astype(BF16)
    return high, (values - high.astype(F32)).astype(BF16)


def pack_small(norm, conv, bias, gate, heads, n, rows):
    conv_rows = conv.reshape(CONV, n, CH // n).transpose(1, 0, 2).reshape(n, -1)
    small = jnp.concatenate(
        [norm.reshape(n, -1), conv_rows, bias.reshape(n, -1), gate.reshape(n, -1)], axis=1
    )
    small = jnp.pad(small, ((0, 0), (0, rows * SMALL - small.shape[1])))
    heads = jnp.broadcast_to(heads[None], (n, heads.shape[0]))
    heads = jnp.pad(heads, ((0, 0), (0, rows * SMALL - heads.shape[1])))
    extra = [item.reshape(n, rows, SMALL) for item in (*high_low(small), *high_low(heads))]
    before = jnp.zeros((n, rows, PROJ - WIDE + 128), BF16)
    after = jnp.zeros((n, rows, WIDE - PROJ - 4 * SMALL), BF16)
    return jnp.concatenate([before, *extra, after], axis=2)


def body(
    inputs,
    cotangent,
    seq_lengths,
    norm_gain,
    in_weight,
    conv_weight,
    conv_bias,
    dt_bias,
    a_log,
    skip_gain,
    gate_gain,
    out_weight,
):
    section = lax.axis_index("section")
    is_first = section == 0
    n = lax.axis_size("dp")
    rows = in_weight.shape[1]
    pack, norm_all, conv_all, bias_all, gate_all = gather_weights(
        in_weight[0], out_weight[0], norm_gain[0], conv_weight[0], conv_bias[0], gate_gain[0]
    )
    spare = ROWS - H
    params = (
        norm_all,
        conv_all,
        bias_all,
        jnp.pad(dt_bias.astype(F32), ((0, 0), (0, spare))),
        jnp.pad(-jnp.exp(a_log.astype(F32)), ((0, 0), (0, spare))),
        jnp.repeat(skip_gain.astype(F32), DI // H, axis=1),
        gate_all,
    )

    def pick(first, second):
        return jnp.where(is_first, first, second)

    out1, _, _ = run_layer(False, seq_lengths[0], inputs[0], cotangent[0], params, pack)
    lens2 = pick(seq_lengths[1], seq_lengths[0])
    came = pass_section(out1, 1)
    two = run_layer(True, lens2, pick(inputs[1], came), cotangent[0], params, pack)
    lens3 = pick(seq_lengths[0], seq_lengths[1])
    came = pass_section(two[1], 1)
    pulled = pass_section(two[3], -1)
    three = run_layer(
        True, lens3, pick(inputs[0], came), pick(pulled, cotangent[1]), params, pack
    )
    pulled = pass_section(three[3], -1)
    four = run_layer(True, seq_lengths[1], inputs[1], pulled, params, pack)

    section_outputs = jnp.stack(
        [pick(three[1].astype(F32), two[0]), pick(two[1].astype(F32), three[0])]
    )
    input_grads = jnp.stack(
        [pick(three[2], two[3].astype(F32)), pick(four[2], three[3].astype(F32))]
    )

    active = jnp.arange(ROWS)[:, None] < jnp.sum(seq_lengths[1])
    branch_grad = pick(jnp.where(active, pulled, jnp.zeros_like(pulled)), two[6])
    grad_out = jnp.einsum(
        "tf,td->fd",
        jnp.concatenate([two[5], three[5]]),
        jnp.concatenate([branch_grad, three[6]]),
        preferred_element_type=F32,
    ).astype(BF16)
    got_out = lax.all_to_all(grad_out.reshape(n, 2 * rows, D), "dp", 0, 0)

    smalls = [pick(four[i], two[i]) + three[i] for i in range(8, 15)]
    norm_s, conv_s, bias_s, gate_s, skip_s, dtb_s, rate_s = smalls
    heads = jnp.concatenate(
        [dtb_s[0, :H], rate_s[0, :H], jnp.sum(skip_s.reshape(H, DI // H), axis=1)]
    )
    extra = pack_small(norm_s, conv_s, bias_s, gate_s, heads, n, rows)
    grad_in = in_grad(two[4], three[4], pick(four[7], two[7]), three[7], extra)
    got_in = lax.all_to_all(grad_in, "dp", 0, 0)
    sum_out = jnp.sum(got_out.astype(F32), axis=0)
    sum_in = jnp.sum(got_in.astype(F32), axis=0)
    own = [sum_in[:, PROJ + i * SMALL : PROJ + (i + 1) * SMALL].reshape(-1) for i in range(4)]
    flat, heads = own[0] + own[1], own[2] + own[3]
    norm_g, conv_g, bias_g, gate_g = [flat[a:b] for a, b in small_cuts(n)]
    return (
        section_outputs[None],
        input_grads[None],
        norm_g[None],
        sum_in[None, :, :PROJ],
        conv_g.reshape(1, CONV, -1),
        bias_g[None],
        heads[None, :H],
        heads[None, H : 2 * H],
        heads[None, 2 * H : 3 * H],
        gate_g[None],
        sum_out[None],
    )


def solution(mesh):
    in_specs = (
        P(None, "dp", None),
        P(None, "dp", None),
        P(None, "dp"),
        P("section", "dp"),
        P("section", "dp", None),
        P("section", None, "dp"),
        P("section", "dp"),
        P("section", None),
        P("section", None),
        P("section", None),
        P("section", "dp"),
        P("section", "dp", None),
    )
    out_specs = (
        P("section", None, "dp", None),
        P("section", None, "dp", None),
        P("section", "dp"),
        P("section", "dp", None),
        P("section", None, "dp"),
        P("section", "dp"),
        P("section", None),
        P("section", None),
        P("section", None),
        P("section", "dp"),
        P("section", "dp", None),
    )
    return jax.shard_map(body, mesh=mesh, in_specs=in_specs, out_specs=out_specs, check_vma=False)
```

```python
import functools

import jax
import jax.numpy as jnp
from jax import lax
from jax.experimental import pallas as pl
from jax.experimental.pallas import tpu as pltpu
from jax.sharding import PartitionSpec as P

H = 32
CONV = 4
D = 1024
DI = 2048
CH = 2304
PROJ = 4384
ROWS = 128
WIDE = 4480
PACK = WIDE + 2 * D
EPS = 1e-05
PRECISE = lax.Precision.HIGHEST
F32 = jnp.float32
BF16 = jnp.bfloat16
VMEM_LIMIT = 50 * 1024 * 1024


def swap_section(block):
    return lax.ppermute(block, "section", [(0, 1), (1, 0)])


def pass_section(block, distance):
    devices = range(lax.axis_size("section"))
    route = [(i - distance, i) for i in devices if i - distance in devices]
    return lax.ppermute(block, "section", route)


def sub_sizes(n):
    side = round(n ** (1 / 3))
    return (side, side, side) if side**3 == n else (n, 1, 1)


def axis_stride(axis, sizes):
    stride = 1
    for size in sizes[axis + 1 :]:
        stride *= size
    return stride


def place(axis, sizes):
    return lax.rem(lax.axis_index("dp") // axis_stride(axis, sizes), sizes[axis])


def hop(block, axis, sizes, target):
    stride, size = axis_stride(axis, sizes), sizes[axis]
    n = lax.axis_size("dp")
    route = []
    for section in range(lax.axis_size("section")):
        for d in range(n):
            at = d // stride % size
            route.append((section * n + d, section * n + d + (target(section, at) - at) * stride))
    return lax.ppermute(block, ("section", "dp"), route)


def ring_reduce(block, axis, dim, sizes, total=None, start=0, stop=None):
    size = sizes[axis]
    turn = 1 - 2 * lax.axis_index("section")
    at = place(axis, sizes)

    def chunk(step):
        index = jnp.mod(at - turn * (1 + step), size)
        return lax.dynamic_index_in_dim(block, index, dim, keepdims=False)

    total = chunk(0) if total is None else total
    for step in range(start, size - 1 if stop is None else stop):
        came = hop(total, axis, sizes, lambda s, c: (c + 1 - 2 * s) % size)
        total = (came.astype(F32) + chunk(step + 1).astype(F32)).astype(BF16)
    return total


def direct_reduce(block, axis, dim, sizes, last=False):
    size = sizes[axis]
    at = place(axis, sizes)

    def chunk(away):
        return lax.dynamic_index_in_dim(block, jnp.mod(at + away, size), dim, keepdims=False)

    came = [hop(chunk(k), axis, sizes, lambda s, c: (c + k) % size) for k in range(1, size)]
    total = sum((item.astype(F32) for item in came), chunk(0).astype(F32))
    return total if last else total.astype(BF16)


def dot_nt(left, right, precision=None):
    return lax.dot_general(
        left, right, (((1,), (1,)), ((), ())), precision=precision, preferred_element_type=F32
    )


def dot_tn(left, right, precision=None):
    return lax.dot_general(
        left, right, (((0,), (0,)), ((), ())), precision=precision, preferred_element_type=F32
    )


def column_iota(shape, axis):
    return lax.broadcasted_iota(jnp.int32, shape, axis)


def lag_masks(first, filled):
    at = column_iota((ROWS, 1), 0)
    own = (at >= first).astype(jnp.int32) + (at >= filled).astype(jnp.int32)
    masks = []
    for lag in range(1, CONV):
        earlier = (at - lag >= first).astype(jnp.int32) + (at - lag >= filled).astype(jnp.int32)
        masks.append(((at >= lag) & (earlier == own)).astype(F32))
    return masks


def pair_mask(first, filled):
    i = column_iota((ROWS, ROWS), 0)
    j = column_iota((ROWS, ROWS), 1)
    seg_i = (i >= first).astype(jnp.int32) + (i >= filled).astype(jnp.int32)
    seg_j = (j >= first).astype(jnp.int32) + (j >= filled).astype(jnp.int32)
    return (i >= j) & (seg_i == seg_j)


IN_CHUNKS = tuple((start, 512) for start in range(0, 4096, 512)) + ((4096, 384),)


def layer_kernel(
    mode,
    lens_ref,
    v_ref,
    dout_ref,
    norm_ref,
    taps_ref,
    bias_ref,
    dtb_ref,
    rate_ref,
    skip_ref,
    gate_ref,
    pack_ref,
    *rest,
):
    rest = list(rest)
    with_back = mode != "forward"
    with_front = mode != "back"
    if mode == "back":
        zx, ys = rest.pop(0), rest.pop(0)
        dv_ref, dzx_ref = rest.pop(0), rest.pop(0)
    elif mode == "forward":
        outb_ref, nb_ref, gn_ref = [rest.pop(0) for _ in range(3)]
    else:
        out_ref, outb_ref, dv_ref, dvb_ref, nb_ref, gn_ref, gb_ref, dzx_ref = [
            rest.pop(0) for _ in range(8)
        ]
    if with_back:
        dnorm_ref, dtaps_ref, dbias_ref, dgate_ref, dskip_ref, ddtb_ref, drate_ref = [
            rest.pop(0) for _ in range(7)
        ]
    if mode == "keep":
        zx, ys = rest.pop(0), rest.pop(0)
    win, wout, sems, xc, gs, cum_t, dt_t = [rest.pop(0) for _ in range(7)]
    if mode in ("forward", "both"):
        zx, ys = rest.pop(0), rest.pop(0)
    if with_back:
        slope, decay, dgs, dxc, row_part, col_part, dscore = [rest.pop(0) for _ in range(7)]
    if mode == "back":
        gb_ref = rest.pop(0)
    blocks = win.shape[0]
    quarter = blocks // 4
    block_rows = win.shape[1]

    copies = [
        pltpu.make_async_copy(
            pack_ref.at[:, :, pl.ds(start, size)], win.at[:, :, pl.ds(start, size)], sems.at[k]
        )
        for k, (start, size) in enumerate(IN_CHUNKS)
    ]
    for half in range(2):
        copies.append(
            pltpu.make_async_copy(
                pack_ref.at[:, :, pl.ds(WIDE + half * D, D)],
                wout.at[:, pl.ds(half * block_rows, block_rows), :],
                sems.at[len(IN_CHUNKS) + half],
            )
        )
    for copy in copies if with_front else copies[len(IN_CHUNKS) :] + copies[: len(IN_CHUNKS)]:
        copy.start()

    first = lens_ref[0]
    filled = lens_ref[0] + lens_ref[1]
    masks = lag_masks(first, filled)
    active = (column_iota((ROWS, 1), 0) < filled).astype(F32)
    lane = column_iota((ROWS, ROWS), 1)
    low_lanes = lane < 64
    head_lanes = lane < H

    v = v_ref[...].astype(F32)
    r = lax.rsqrt(jnp.mean(v * v, axis=1, keepdims=True) + EPS)
    if with_front:
        nb_ref[...] = (v * r * norm_ref[...]).astype(BF16)

        for k, (start, size) in enumerate(IN_CHUNKS):
            copies[k].wait()
            zx[:, pl.ds(start, size)] = jnp.dot(
                nb_ref[...],
                win[:, :, pl.ds(start, size)].reshape(D, size),
                preferred_element_type=F32,
            )

    def conv_step(c, carry):
        at = pl.ds(pl.multiple_of(c * 256, 256), 256)
        u = zx[:, pl.ds(pl.multiple_of(DI + c * 256, 256), 256)]
        taps = taps_ref[:, at]
        total = bias_ref[:, at] + taps[CONV - 1 : CONV] * u
        for lag in range(1, CONV):
            total += taps[CONV - 1 - lag : CONV - lag] * (pltpu.roll(u, lag, 0) * masks[lag - 1])
        sig = jax.nn.sigmoid(total)
        xc[:, at] = total * sig
        if with_back:
            slope[:, at] = sig * (1.0 + total * (1.0 - sig))
        return carry

    lax.fori_loop(0, CH // 256, conv_step, 0)

    raw = jnp.where(head_lanes, zx[:, DI + CH :], 0.0) + dtb_ref[...]
    dt = jnp.maximum(raw, 0.0) + jnp.log1p(jnp.exp(-jnp.abs(raw)))
    dt = jnp.where(head_lanes, dt, 0.0)
    rate = rate_ref[...]
    lower = (column_iota((ROWS, ROWS), 0) >= lane).astype(F32)
    cum = jnp.dot(lower, dt * rate, precision=PRECISE, preferred_element_type=F32)
    cum_t[...] = cum.T
    dt_t[...] = dt.T
    allowed = pair_mask(first, filled)
    bb = xc[:, DI : DI + 128]
    cc = xc[:, DI + 128 :]
    score = dot_nt(cc, bb, PRECISE)

    def head_group(g, carry):
        turned = pltpu.roll(cum, lax.rem(ROWS - 8 * g, ROWS), 1)
        rows = pl.ds(pl.multiple_of(g * 8, 8), 8)
        cum_rows = cum_t[rows, :]
        dt_rows = dt_t[rows, :]
        for pair in range(4):
            at = pl.ds(pl.multiple_of(g * 512 + pair * 128, 128), 128)
            mixes = []
            for k in (2 * pair, 2 * pair + 1):
                gap = turned[:, k : k + 1] - cum_rows[k : k + 1, :]
                fade = jnp.exp(jnp.where(allowed, gap, -1e30))
                if with_back:
                    decay[g * 8 + k] = fade
                if with_front:
                    mixes.append((score * fade * dt_rows[k : k + 1, :]).astype(BF16))
            if not with_front:
                continue
            x = xc[:, at]
            halves = [jnp.where(low_lanes, x, 0.0), jnp.where(low_lanes, 0.0, x)]
            ys[:, at] = (
                jnp.dot(
                    jnp.concatenate(mixes, axis=1),
                    jnp.concatenate(halves, axis=0).astype(BF16),
                    preferred_element_type=F32,
                )
                + skip_ref[:, at] * x
            )
        return carry

    lax.fori_loop(0, H // 8, head_group, 0)

    def gate_step(c, total):
        at = pl.ds(pl.multiple_of(c * 256, 256), 256)
        z = zx[:, at]
        g = ys[:, at] * (z * jax.nn.sigmoid(z))
        gs[:, at] = g
        return total + jnp.sum(g * g, axis=1, keepdims=True)

    total = lax.fori_loop(0, DI // 256, gate_step, jnp.zeros((ROWS, 1), F32))
    q = lax.rsqrt(total * (1.0 / DI) + EPS)

    if with_front:

        def gain_step(c, carry):
            at = pl.ds(pl.multiple_of(c * 256, 256), 256)
            gn_ref[:, at] = (gs[:, at] * q * gate_ref[:, at]).astype(BF16)
            return carry

        lax.fori_loop(0, DI // 256, gain_step, 0)

    for copy in copies[len(IN_CHUNKS) :]:
        copy.wait()

    if with_front:

        def branch_step(c, carry):
            at = pl.ds(pl.multiple_of(c * 512, 512), 512)
            branch = jnp.dot(
                gn_ref[...], wout[:, :, at].reshape(DI, 512), preferred_element_type=F32
            )
            result = v_ref[:, at].astype(F32) + active * branch
            outb_ref[:, at] = result.astype(BF16)
            if with_back:
                out_ref[:, at] = result
            return carry

        lax.fori_loop(0, D // 512, branch_step, 0)

    if not with_back:
        return

    gb_ref[...] = (active * dout_ref[...].astype(F32)).astype(BF16)

    def dgate_step(c, total):
        at = pl.ds(pl.multiple_of(c * 512, 512), 512)
        weight = wout[pl.ds(c * quarter, quarter)].reshape(512, D)
        dgn = dot_nt(gb_ref[...], weight)
        g = gs[:, at]
        dgate_ref[:, at] = jnp.sum(dgn * (g * q), axis=0, keepdims=True)
        pulled = dgn * gate_ref[:, at]
        dgs[:, at] = pulled
        return total + jnp.sum(pulled * g, axis=1, keepdims=True)

    total = lax.fori_loop(0, 4, dgate_step, jnp.zeros((ROWS, 1), F32))
    pull = q * q * q * (total * (1.0 / DI))

    def dz_step(c, carry):
        at = pl.ds(pl.multiple_of(c * 256, 256), 256)
        dg = q * dgs[:, at] - gs[:, at] * pull
        z = zx[:, at]
        sig = jax.nn.sigmoid(z)
        dy = dg * (z * sig)
        dgs[:, at] = dy
        dzx_ref[:, at] = (dg * ys[:, at] * (sig * (1.0 + z * (1.0 - sig)))).astype(BF16)
        dskip_ref[:, at] = jnp.sum(dy * xc[:, at], axis=0, keepdims=True)
        return carry

    lax.fori_loop(0, DI // 256, dz_step, 0)

    row_part[...] = jnp.zeros((ROWS, ROWS), F32)
    col_part[...] = jnp.zeros((ROWS, ROWS), F32)
    dscore[...] = jnp.zeros((ROWS, ROWS), F32)

    def head_back(g, carry):
        rows = pl.ds(pl.multiple_of(g * 8, 8), 8)
        dt_rows = dt_t[rows, :]
        col_sums = []
        row_sum = row_part[...]
        dscore_sum = dscore[...]
        for pair in range(4):
            at = pl.ds(pl.multiple_of(g * 512 + pair * 128, 128), 128)
            dy = dgs[:, at]
            dys = jnp.concatenate(
                [jnp.where(low_lanes, dy, 0.0), jnp.where(low_lanes, 0.0, dy)], axis=0
            ).astype(BF16)
            dmix = dot_nt(dys, xc[:, at].astype(BF16))
            mixes = []
            for side in range(2):
                k = 2 * pair + side
                dt_row = dt_rows[k : k + 1, :]
                fade = decay[g * 8 + k]
                part = dmix[side * ROWS : (side + 1) * ROWS] * fade
                dscore_sum += part * dt_row
                part = part * score
                col_sums.append(jnp.sum(part, axis=0, keepdims=True))
                row_sum += jnp.where(
                    lane == g * 8 + k, jnp.sum(part * dt_row, axis=1, keepdims=True), 0.0
                )
                mixes.append((score * fade * dt_row).astype(BF16))
            dxc[:, at] = dot_tn(jnp.concatenate(mixes, axis=0), dys) + skip_ref[:, at] * dy
        col_part[rows, :] = jnp.concatenate(col_sums, axis=0)
        row_part[...] = row_sum
        dscore[...] = dscore_sum
        return carry

    lax.fori_loop(0, H // 8, head_back, 0)

    col_sum = col_part[...].T
    dcum = row_part[...] - dt * col_sum
    dlog = dot_tn(lower, dcum, PRECISE)
    drate_ref[...] = jnp.sum(dlog * dt, axis=0, keepdims=True) * rate
    draw = jnp.where(head_lanes, (col_sum + dlog * rate) * jax.nn.sigmoid(raw), 0.0)
    ddtb_ref[...] = jnp.sum(draw, axis=0, keepdims=True)
    dzx_ref[:, DI + CH :] = draw.astype(BF16)
    dxc[:, DI : DI + 128] = dot_tn(dscore[...], cc, PRECISE)
    dxc[:, DI + 128 :] = jnp.dot(dscore[...], bb, precision=PRECISE, preferred_element_type=F32)

    def dconv_step(c, carry):
        at = pl.ds(pl.multiple_of(c * 256, 256), 256)
        wide_at = pl.ds(pl.multiple_of(DI + c * 256, 256), 256)
        u = zx[:, wide_at]
        taps = taps_ref[:, at]
        dconv = dxc[:, at] * slope[:, at]
        dbias_ref[:, at] = jnp.sum(dconv, axis=0, keepdims=True)
        du = taps[CONV - 1 : CONV] * dconv
        dtaps_ref[CONV - 1 : CONV, at] = jnp.sum(dconv * u, axis=0, keepdims=True)
        for lag in range(1, CONV):
            masked = dconv * masks[lag - 1]
            k = CONV - 1 - lag
            dtaps_ref[k : k + 1, at] = jnp.sum(
                masked * pltpu.roll(u, lag, 0), axis=0, keepdims=True
            )
            du += taps[k : k + 1] * pltpu.roll(masked, ROWS - lag, 0)
        dzx_ref[:, wide_at] = du.astype(BF16)
        return carry

    lax.fori_loop(0, CH // 256, dconv_step, 0)

    if not with_front:
        for copy in copies[: len(IN_CHUNKS)]:
            copy.wait()

    def dnorm_step(c, total):
        at = pl.ds(pl.multiple_of(c * 256, 256), 256)
        weight = win[pl.ds(c * quarter, quarter)].reshape(256, WIDE)
        dnormed = dot_nt(dzx_ref[...], weight)
        vc = v_ref[:, at].astype(F32)
        dnorm_ref[:, at] = jnp.sum(dnormed * (vc * r), axis=0, keepdims=True)
        pulled = dnormed * norm_ref[:, at]
        dv_ref[:, at] = pulled
        return total + jnp.sum(pulled * vc, axis=1, keepdims=True)

    total = lax.fori_loop(0, 4, dnorm_step, jnp.zeros((ROWS, 1), F32))
    pull = r * r * r * (total * (1.0 / D))

    def dv_step(c, carry):
        at = pl.ds(pl.multiple_of(c * 256, 256), 256)
        result = (
            dout_ref[:, at].astype(F32) + r * dv_ref[:, at] - v_ref[:, at].astype(F32) * pull
        )
        dv_ref[:, at] = result
        if with_front:
            dvb_ref[:, at] = result.astype(BF16)
        return carry

    lax.fori_loop(0, D // 256, dv_step, 0)


def run_layer(mode, lens, v, dout, params, pack, kept=()):
    blocks, block_rows = pack.shape[0], pack.shape[1]
    vmem = pl.BlockSpec(memory_space=pltpu.VMEM)
    shape = jax.ShapeDtypeStruct
    smalls = [
        shape((1, D), F32),
        shape((CONV, CH), F32),
        shape((1, CH), F32),
        shape((1, DI), F32),
        shape((1, DI), F32),
        shape((1, ROWS), F32),
        shape((1, ROWS), F32),
    ]
    if mode == "forward":
        outs = [shape((ROWS, D), BF16), shape((ROWS, D), BF16), shape((ROWS, DI), BF16)]
    elif mode == "back":
        outs = [shape((ROWS, D), F32), shape((ROWS, WIDE), BF16), *smalls]
    else:
        outs = [
            shape((ROWS, D), F32),
            shape((ROWS, D), BF16),
            shape((ROWS, D), F32),
            shape((ROWS, D), BF16),
            shape((ROWS, D), BF16),
            shape((ROWS, DI), BF16),
            shape((ROWS, D), BF16),
            shape((ROWS, WIDE), BF16),
            *smalls,
        ]
    if mode == "keep":
        outs += [shape((ROWS, WIDE), F32), shape((ROWS, DI), F32)]
    scratch = [
        pltpu.VMEM((blocks, block_rows, WIDE), BF16),
        pltpu.VMEM((blocks, 2 * block_rows, D), BF16),
        pltpu.SemaphoreType.DMA((len(IN_CHUNKS) + 2,)),
        pltpu.VMEM((ROWS, CH), F32),
        pltpu.VMEM((ROWS, DI), F32),
        pltpu.VMEM((ROWS, ROWS), F32),
        pltpu.VMEM((ROWS, ROWS), F32),
    ]
    if mode in ("forward", "both"):
        scratch += [pltpu.VMEM((ROWS, WIDE), F32), pltpu.VMEM((ROWS, DI), F32)]
    if mode != "forward":
        scratch += [
            pltpu.VMEM((ROWS, CH), F32),
            pltpu.VMEM((H, ROWS, ROWS), F32),
            pltpu.VMEM((ROWS, DI), F32),
            pltpu.VMEM((ROWS, CH), F32),
            pltpu.VMEM((ROWS, ROWS), F32),
            pltpu.VMEM((ROWS, ROWS), F32),
            pltpu.VMEM((ROWS, ROWS), F32),
        ]
    if mode == "back":
        scratch += [pltpu.VMEM((ROWS, D), BF16)]
    flops = 2 * ROWS * (WIDE * D + DI * D) * (2 if mode in ("both", "keep") else 1)
    return pl.pallas_call(
        functools.partial(layer_kernel, mode),
        out_shape=outs,
        in_specs=[pl.BlockSpec(memory_space=pltpu.SMEM)]
        + [vmem] * 9
        + [pl.BlockSpec(memory_space=pl.ANY)]
        + [vmem] * len(kept),
        out_specs=[vmem] * len(outs),
        scratch_shapes=scratch,
        cost_estimate=pl.CostEstimate(
            flops=flops, bytes_accessed=D * PACK * 2, transcendentals=H * ROWS * ROWS
        ),
        compiler_params=pltpu.CompilerParams(vmem_limit_bytes=VMEM_LIMIT),
        name="layer_" + mode,
    )(lens, v, dout, *params, pack, *kept)


GRAD_CHUNK = 896
COLORS = ((0, 2), (2, 2), (4, 1))
SPARE_AT = PROJ - WIDE + 128


def in_grad_kernel(last, first_ref, second_ref, dzx_ref, dzx2_ref, extra_ref, out_ref, turned):
    @pl.when(pl.program_id(0) == 0)
    def _():
        turned[:, :ROWS] = first_ref[...].T
        turned[:, ROWS:] = second_ref[...].T

    both = jnp.concatenate([dzx_ref[...], dzx2_ref[...]], axis=0)
    grad = jnp.dot(turned[...], both, preferred_element_type=F32)
    if not last:
        out_ref[...] = grad.astype(BF16).reshape(out_ref.shape)
        return
    head = GRAD_CHUNK - 128
    out_ref[:, :, :head] = grad[:, :head].astype(BF16).reshape(extra_ref.shape[:2] + (head,))
    tail = grad[:, head:].reshape(extra_ref.shape)
    spare = lax.broadcasted_iota(jnp.int32, extra_ref.shape, 2) >= PROJ - WIDE + 128
    out_ref[:, :, head:] = jnp.where(spare, extra_ref[...], tail).astype(BF16)


def in_grad(color, first, second, dzx, dzx2, extra):
    blocks, block_rows = extra.shape[0], extra.shape[1]
    start, count = COLORS[color]
    return pl.pallas_call(
        functools.partial(in_grad_kernel, color == len(COLORS) - 1),
        grid=(count,),
        out_shape=jax.ShapeDtypeStruct((blocks, block_rows, count * GRAD_CHUNK), BF16),
        in_specs=[
            pl.BlockSpec((ROWS, D), lambda i: (0, 0)),
            pl.BlockSpec((ROWS, D), lambda i: (0, 0)),
            pl.BlockSpec((ROWS, GRAD_CHUNK), lambda i: (0, i + start)),
            pl.BlockSpec((ROWS, GRAD_CHUNK), lambda i: (0, i + start)),
            pl.BlockSpec((blocks, block_rows, 128), lambda i: (0, 0, 0)),
        ],
        out_specs=pl.BlockSpec((blocks, block_rows, GRAD_CHUNK), lambda i: (0, 0, i)),
        scratch_shapes=[pltpu.VMEM((D, 2 * ROWS), BF16)],
        cost_estimate=pl.CostEstimate(
            flops=4 * ROWS * D * count * GRAD_CHUNK,
            bytes_accessed=D * count * GRAD_CHUNK * 2,
            transcendentals=0,
        ),
        compiler_params=pltpu.CompilerParams(vmem_limit_bytes=VMEM_LIMIT),
        name="in_weight_grad",
    )(first, second, dzx, dzx2, extra)


def out_grad_kernel(gn_ref, gn2_ref, gb_ref, gb2_ref, out_ref):
    left = jnp.concatenate([gn_ref[...], gn2_ref[...]], axis=0)
    right = jnp.concatenate([gb_ref[...], gb2_ref[...]], axis=0)
    blocks, block_rows = out_ref.shape[0], out_ref.shape[1]
    grad = dot_tn(left, right).astype(BF16).reshape(blocks, 2 * block_rows, D)
    out_ref[:, :, :D] = grad[:, :block_rows]
    out_ref[:, :, D:] = grad[:, block_rows:]


def out_grad(gn, gn2, gb, gb2, blocks, block_rows):
    return pl.pallas_call(
        out_grad_kernel,
        grid=(4,),
        out_shape=jax.ShapeDtypeStruct((blocks, block_rows, 2 * D), BF16),
        in_specs=[
            pl.BlockSpec((ROWS, DI // 4), lambda i: (0, i)),
            pl.BlockSpec((ROWS, DI // 4), lambda i: (0, i)),
            pl.BlockSpec((ROWS, D), lambda i: (0, 0)),
            pl.BlockSpec((ROWS, D), lambda i: (0, 0)),
        ],
        out_specs=pl.BlockSpec((blocks // 4, block_rows, 2 * D), lambda i: (i, 0, 0)),
        cost_estimate=pl.CostEstimate(
            flops=4 * ROWS * D * DI, bytes_accessed=D * DI * 2, transcendentals=0
        ),
        compiler_params=pltpu.CompilerParams(vmem_limit_bytes=VMEM_LIMIT),
        name="out_weight_grad",
    )(gn, gn2, gb, gb2)


def spread(row, blocks):
    width = row.shape[1]
    each = width // blocks
    block = column_iota((blocks, width), 0)
    at = column_iota((blocks, width), 1)
    own = (at >= block * each) & (at < block * each + each)
    fold = lax.rem(column_iota((width, 128), 0), each) + SPARE_AT == column_iota((width, 128), 1)
    return jnp.dot(
        jnp.where(own, row, 0.0).astype(BF16), fold.astype(BF16), preferred_element_type=F32
    )


def extras_kernel(section_ref, *refs):
    out_ref = refs[21]
    is_first = section_ref[0] == 0
    norm, taps, bias, gate, skip, dtb, rate = [
        jnp.where(is_first, refs[i][...], refs[i + 7][...]) + refs[i + 14][...] for i in range(7)
    ]
    blocks = out_ref.shape[0]
    out_ref[...] = jnp.zeros(out_ref.shape, F32)
    for k in range(CONV):
        out_ref[:, k, :] = spread(taps[k : k + 1], blocks)
    out_ref[:, 4, :] = spread(bias, blocks)
    out_ref[:, 5, :] = spread(norm, blocks)
    out_ref[:, 6, :] = spread(gate, blocks)
    owner = column_iota((DI, 128), 0) // (DI // H) + SPARE_AT + 2 * H
    fold = (owner == column_iota((DI, 128), 1)).astype(F32)
    heads = jnp.dot(
        jnp.broadcast_to(skip, (8, DI)), fold, precision=PRECISE, preferred_element_type=F32
    )[:1]
    lane = column_iota((1, 128), 1)
    heads = jnp.where(lane < SPARE_AT + 2 * H, pltpu.roll(rate, SPARE_AT + H, 1), heads)
    heads = jnp.where(lane < SPARE_AT + H, pltpu.roll(dtb, SPARE_AT, 1), heads)
    out_ref[:, 7, :] = jnp.broadcast_to(heads, (blocks, 128))


def pack_extras(section, lists, blocks, block_rows):
    vmem = pl.BlockSpec(memory_space=pltpu.VMEM)
    return pl.pallas_call(
        extras_kernel,
        out_shape=jax.ShapeDtypeStruct((blocks, block_rows, 128), F32),
        in_specs=[pl.BlockSpec(memory_space=pltpu.SMEM)] + [vmem] * 21,
        out_specs=vmem,
        compiler_params=pltpu.CompilerParams(vmem_limit_bytes=VMEM_LIMIT),
        name="small_grads",
    )(section.reshape(1).astype(jnp.int32), *lists)


def pack_kernel(in_ref, out_ref, norm_ref, conv_ref, bias_ref, gate_ref, pack_ref, line):
    rows = in_ref.shape[0]
    edge = WIDE - 128
    pack_ref[:, :edge] = in_ref[:, :edge]
    line[...] = jnp.zeros(line.shape, F32)
    line[:CONV, : conv_ref.shape[1]] = conv_ref[...].astype(F32)
    for k, ref in ((4, bias_ref), (5, norm_ref), (6, gate_ref)):
        line[k : k + 1, : ref.shape[1]] = ref[...].astype(F32)
    small = pltpu.roll(line[...], SPARE_AT, 1)
    line[:, :SPARE_AT] = in_ref[:, edge:].astype(F32)
    mixed = jnp.where(column_iota(line.shape, 1) < SPARE_AT, line[...], small)
    pack_ref[:, edge:WIDE] = mixed.astype(BF16)
    pack_ref[:, WIDE : WIDE + D] = out_ref[:rows]
    pack_ref[:, WIDE + D :] = out_ref[rows:]


def gather_weights(in_shard, out_shard, norm, conv, bias, gate):
    rows = in_shard.shape[0]
    n = lax.axis_size("dp")
    vmem = pl.BlockSpec(memory_space=pltpu.VMEM)
    pack = pl.pallas_call(
        pack_kernel,
        out_shape=jax.ShapeDtypeStruct((rows, PACK), BF16),
        in_specs=[vmem] * 6,
        out_specs=vmem,
        scratch_shapes=[pltpu.VMEM((rows, 128), F32)],
        name="pack_shards",
    )(in_shard, out_shard, norm[None], conv, bias[None], gate[None])
    whole = lax.all_gather(pack, "dp", axis=0, tiled=False)
    small = whole[:, :, PROJ:WIDE].astype(F32)

    def unite(k, size):
        return small[:, k, : size // n].reshape(1, size)

    conv_all = jnp.concatenate([unite(k, CH) for k in range(CONV)])
    return whole, unite(5, D), conv_all, unite(4, CH), unite(6, DI)


def body(
    inputs,
    cotangent,
    seq_lengths,
    norm_gain,
    in_weight,
    conv_weight,
    conv_bias,
    dt_bias,
    a_log,
    skip_gain,
    gate_gain,
    out_weight,
):
    section = lax.axis_index("section")
    is_first = section == 0
    n = lax.axis_size("dp")
    rows = in_weight.shape[1]
    pack, norm_all, conv_all, bias_all, gate_all = gather_weights(
        in_weight[0], out_weight[0], norm_gain[0], conv_weight[0], conv_bias[0], gate_gain[0]
    )
    spare = ROWS - H
    params = (
        norm_all,
        conv_all,
        bias_all,
        jnp.pad(dt_bias.astype(F32), ((0, 0), (0, spare))),
        jnp.pad(-jnp.exp(a_log.astype(F32)), ((0, 0), (0, spare))),
        jnp.repeat(skip_gain.astype(F32), DI // H, axis=1),
        gate_all,
    )

    def pick(first, second):
        return jnp.where(is_first, first, second)

    out1, _, _ = run_layer("forward", seq_lengths[0], inputs[0], cotangent[0], params, pack)
    lens2 = pick(seq_lengths[1], seq_lengths[0])
    came = pass_section(out1, 1)
    two = run_layer("keep", lens2, pick(inputs[1], came), cotangent[0], params, pack)
    lens3 = pick(seq_lengths[0], seq_lengths[1])
    came = swap_section(pick(two[1], two[3]))
    three = run_layer(
        "both", lens3, pick(inputs[0], came), pick(came, cotangent[1]), params, pack
    )
    pulled = pass_section(three[3], -1)

    sizes = sub_sizes(n)
    cube = (*sizes, rows)
    active = jnp.arange(ROWS)[:, None] < jnp.sum(seq_lengths[1])
    branch_grad = pick(jnp.where(active, pulled, jnp.zeros_like(pulled)), two[6])
    part_out = out_grad(two[5], three[5], branch_grad, three[6], n, rows)
    pulled, part_out = lax.optimization_barrier((pulled, part_out))
    part_out = part_out.reshape(*cube, -1)
    total_out = ring_reduce(part_out, 2, 2, sizes, None, 0, 1)

    four = run_layer("back", seq_lengths[1], inputs[1], pulled, params, pack, two[15:17])

    section_outputs = jnp.stack(
        [pick(three[1].astype(F32), two[0]), pick(two[1].astype(F32), three[0])]
    )
    input_grads = jnp.stack(
        [pick(three[2], two[3].astype(F32)), pick(four[0], three[3].astype(F32))]
    )

    extra = pack_extras(section, (*four[2:9], *two[8:15], *three[8:15]), n, rows)
    dzx, total_out = lax.optimization_barrier((pick(four[1], two[7]), total_out))
    sides = (two[4], three[4], dzx, three[7], extra)
    part_a, part_b, part_c = [
        in_grad(color, *sides).reshape(*cube, -1) for color in range(len(COLORS))
    ]
    part_a = ring_reduce(part_a, 0, 0, sizes)
    part_b = ring_reduce(part_b, 1, 1, sizes)
    part_c = ring_reduce(part_c, 2, 2, sizes)
    part_out = ring_reduce(part_out, 2, 2, sizes, total_out, 1)
    part_c = jnp.concatenate([part_c, part_out], axis=-1)
    wide = part_a.shape[-1]
    part_ab = jnp.concatenate([part_a.swapaxes(0, 1), part_b.swapaxes(0, 1)], axis=-1)
    part_ab = direct_reduce(part_ab, 2, 0, sizes)
    part_c = direct_reduce(part_c, 0, 0, sizes)
    part_ac = jnp.concatenate([part_ab[..., :wide], part_c], axis=-1)
    part_b = direct_reduce(part_ab[..., wide:], 0, 0, sizes, True)
    part_ac = direct_reduce(part_ac, 1, 0, sizes, True)

    spare_at = wide + GRAD_CHUNK - (WIDE - PROJ)
    own_end = wide + GRAD_CHUNK
    sum_in = jnp.concatenate([part_ac[:, :wide], part_b, part_ac[:, wide:spare_at]], axis=1)
    sum_out = jnp.concatenate([part_ac[:, own_end : own_end + D], part_ac[:, own_end + D :]])
    own = part_ac[:, spare_at:own_end]
    heads = own[7]
    return (
        section_outputs[None],
        input_grads[None],
        own[None, 5, : D // n],
        sum_in[None],
        own[None, :CONV, : CH // n],
        own[None, 4, : CH // n],
        heads[None, :H],
        heads[None, H : 2 * H],
        heads[None, 2 * H : 3 * H],
        own[None, 6, : DI // n],
        sum_out[None],
    )


def solution(mesh):
    in_specs = (
        P(None, "dp", None),
        P(None, "dp", None),
        P(None, "dp"),
        P("section", "dp"),
        P("section", "dp", None),
        P("section", None, "dp"),
        P("section", "dp"),
        P("section", None),
        P("section", None),
        P("section", None),
        P("section", "dp"),
        P("section", "dp", None),
    )
    out_specs = (
        P("section", None, "dp", None),
        P("section", None, "dp", None),
        P("section", "dp"),
        P("section", "dp", None),
        P("section", None, "dp"),
        P("section", "dp"),
        P("section", None),
        P("section", None),
        P("section", None),
        P("section", "dp"),
        P("section", "dp", None),
    )
    return jax.shard_map(body, mesh=mesh, in_specs=in_specs, out_specs=out_specs, check_vma=False)
```
